512 devices in a mesh: chan: 64 (over y, z_lo, core), tmpl: 8 (over x, z_hi).
Axes of the slice: x: 4, y: 4, z: 16 (z_hi: 2, z_lo: 8; z = z_hi * 8 + z_lo), core: 2. Of those that a mesh axis runs over, the one named last changes fastest.
Arguments:
- raw_stretches: bfloat16 [4096, 2, 8192], P('chan', None, 'tmpl'), may hold values from -500 to 500
- stretch_ids: int32 [4096], P('chan'), may hold values from -1 to 2047, as said below
- templates: bfloat16 [64, 8, 512, 256], P('chan', 'tmpl'), may hold values from -500 to 500
- offsets: int32 [64, 8], P('chan', 'tmpl'), may hold values from 0 to 63
Outputs:
- detection: float32 [64, 8, 8192], P('chan', None, 'tmpl')
The draws below stay inside these ranges and needn't reach their ends.
Inputs may be any that keep to these rules, and one draw needn't show every extreme that they name: `stretch_ids`: the slots of ingest device i are rows i * 64 to i * 64 + 63. Its stretches fill its first slots in increasing order of stretch id, the rest are -1. Every stretch id appears exactly once; stretch p belongs to channel group p // 32. No ingest device holds two stretches of one channel group, and one ingest device holds a stretch of every channel group.
All inputs are finite; a program needn't handle non-finite values.
Results may differ from the reference program's by a relative error of at most 0.0003.
Values may be sent and summed in bfloat16 or wider, within the bound.
A program may use at most 192 MiB of HBM per device.

```python
import math
import jax
import jax.numpy as jnp
from jax import lax

CH_DEV = 64
TMPL_CH = 512
TMPL_LEN = 256
STRETCHES_GROUP = 32
STRETCH_CH = 2
HOMED = 8
FIBER = 4096
WINDOW = 8192
N_CHAN = 64


def spread_scale(subkey, full_shape, ceiling):
    return jnp.exp(jax.random.uniform(subkey, full_shape, jnp.float32) * math.log(ceiling))


def draw_raw_stretches(key, part):
    key = jax.random.fold_in(key, 11)
    subkeys = jax.random.split(key, 3)
    full_shape = (N_CHAN * N_CHAN, STRETCH_CH, WINDOW)
    row_scale = spread_scale(subkeys[0], (N_CHAN * N_CHAN, STRETCH_CH, 1), 10.0)
    time_scale = spread_scale(subkeys[1], (1, 1, WINDOW), 10.0)
    values = jnp.clip(jax.random.normal(subkeys[2], full_shape, jnp.float32), -4.0, 4.0)
    return (values * row_scale * time_scale).astype(jnp.bfloat16)


def draw_templates(key, part):
    key = jax.random.fold_in(key, 23)
    subkeys = jax.random.split(key, 3)
    full_shape = (N_CHAN, HOMED, TMPL_CH, TMPL_LEN)
    row_scale = spread_scale(subkeys[0], (N_CHAN, HOMED, TMPL_CH, 1), 10.0)
    tap_scale = spread_scale(subkeys[1], (N_CHAN, HOMED, 1, TMPL_LEN), 10.0)
    values = jnp.clip(jax.random.normal(subkeys[2], full_shape, jnp.float32), -4.0, 4.0)
    return (values * row_scale * tap_scale).astype(jnp.bfloat16)


def draw_stretch_ids(key, part):
    key = jax.random.fold_in(key, 37)
    subkeys = jax.random.split(key, 3)
    group_count = N_CHAN
    per_group = N_CHAN // 2
    always_full = jax.random.randint(subkeys[0], (), 0, group_count)
    leaning = jax.random.randint(subkeys[1], (group_count,), 0, 4)
    jitter = jax.random.randint(subkeys[2], (group_count, group_count), 0, 64)
    ingest = jax.lax.broadcasted_iota(jnp.int32, (group_count, group_count), 1)
    priority = (jitter + 16 * leaning[None, :]) * group_count + ingest
    priority = jnp.where(ingest == always_full, 1 << 24, priority)
    unused, chosen = jax.lax.top_k(priority, per_group)
    ranks = jax.lax.broadcasted_iota(jnp.int32, (group_count, per_group, group_count), 1)
    members = jax.lax.broadcasted_iota(jnp.int32, (group_count, per_group, group_count), 2)
    matched = chosen[:, :, None] == members
    places = jnp.sum(jnp.where(matched, ranks + 1, 0), axis=1) - 1
    owner_iota = jax.lax.broadcasted_iota(jnp.int32, (group_count, group_count), 0)
    labels = jnp.where(places >= 0, owner_iota * per_group + places, -1).T
    ordering = jnp.argsort((labels < 0).astype(jnp.int32), axis=1, stable=True)
    packed = jnp.take_along_axis(labels, ordering, axis=1)
    return packed.reshape(-1).astype(jnp.int32)


def place_ends(entries, own_key, low, high):
    place = [jax.random.randint(jax.random.fold_in(own_key, axis), (), 0, length) for axis, length in enumerate(entries.shape)]
    widest = entries.shape.index(max(entries.shape))
    beside = place[:widest] + [(place[widest] + 1) % entries.shape[widest]] + place[widest + 1:]
    return entries.at[tuple(place)].set(low).at[tuple(beside)].set(high)


def setup_inputs(seed: int = 0) -> dict:
    key_of = jax.random.split(jax.random.key(seed), 5)
    return {
        "raw_stretches": draw_raw_stretches(jax.random.fold_in(key_of[4], 71), 0),
        "stretch_ids": draw_stretch_ids(jax.random.fold_in(key_of[4], 71), 0),
        "templates": draw_templates(jax.random.fold_in(key_of[4], 71), 0),
        "offsets": place_ends(jax.random.randint(key_of[3], (N_CHAN, HOMED), 0, CH_DEV), jax.random.fold_in(key_of[3], 1), 0, CH_DEV - 1).astype(jnp.int32),
    }


def correlate_rows(weights, window_rows, length):
    columns = window_rows.shape[1]
    products = jnp.dot(weights.T, window_rows, precision=lax.Precision.HIGHEST)
    flattened = jnp.pad(products.reshape(-1), (0, TMPL_LEN))
    skewed = flattened.reshape(TMPL_LEN, columns + 1)[:, :length]
    return lax.optimization_barrier(jnp.sum(skewed, axis=0))

def reference(raw_stretches, stretch_ids, templates, offsets):
    stretch_total = N_CHAN * STRETCHES_GROUP
    target = jnp.where(stretch_ids >= 0, stretch_ids, stretch_total).astype(jnp.int32)
    fiber_field = jnp.zeros((stretch_total, STRETCH_CH, WINDOW), raw_stretches.dtype).at[target].set(raw_stretches, mode='drop')
    fiber_field = fiber_field.reshape(FIBER, WINDOW).astype(jnp.float32)
    padded = jnp.pad(fiber_field, ((0, TMPL_CH), (0, TMPL_LEN)))
    squares = padded * padded
    sliding = lax.reduce_window(squares, jnp.zeros((), squares.dtype), lax.add, (1, TMPL_LEN), (1, 1), 'VALID')[:, :WINDOW]
    first_rows = (jnp.arange(N_CHAN, dtype=jnp.int32)[:, None] * CH_DEV + offsets).reshape(-1).astype(jnp.int32)
    template_bank = templates.reshape(N_CHAN * HOMED, TMPL_CH, TMPL_LEN)
    volume = float(TMPL_CH * TMPL_LEN)

    def score_one(entry_pair):
        weights, begin_row = entry_pair
        weights = weights.astype(jnp.float32)
        window_rows = lax.dynamic_slice_in_dim(padded, begin_row, TMPL_CH, 0)
        numer = correlate_rows(weights, window_rows, WINDOW)
        energy = lax.optimization_barrier(jnp.sum(lax.dynamic_slice_in_dim(sliding, begin_row, TMPL_CH, 0), axis=0))
        norm_sq = jnp.sum(weights * weights)
        return numer * jnp.sqrt(volume / (jnp.maximum(energy, volume) * norm_sq))
    scores = lax.map(score_one, (template_bank, first_rows))
    return scores.reshape(N_CHAN, HOMED, WINDOW)
```

```python
import functools

import jax
import jax.numpy as jnp
from jax import lax
from jax.experimental import pallas as pl
from jax.experimental.pallas import tpu as pltpu
from jax.sharding import PartitionSpec as P

MESH = pl.DeviceIdType.MESH
F32 = jnp.float32
BF16 = jnp.bfloat16
I32 = jnp.int32
FOLD = 4
LANES = 128


def iota(shape, axis):
    return lax.broadcasted_iota(I32, shape, axis)


def log2(number):
    return number.bit_length() - 1


def kernel(
    chan_count, tmpl_count, run, width, per_group, chunks,
    raw_ref, ids_ref, tmpl_ref, off_ref, out_ref,
    snd1, rcv1, snd2, rcv2, rec, fol, bank, deep, weights, squares, prod, strips, norms, masks,
    s1, r1, s2, r2, st, rt, sz, rz, sf, rf, sr, rr, sq, rq, sn, rn, srf, rrf, sqf, rqf,
):
    rows, segment = raw_ref.shape
    span, taps = tmpl_ref.shape
    group_rows = per_group * width
    reach = span // group_rows
    links = reach // 2
    total_rows = (reach + 1) * group_rows
    pad_rows = deep.shape[0] // FOLD
    columns = deep.shape[1]
    lag = taps // FOLD
    homed = tmpl_count
    classes = chan_count // run
    block1 = run * width
    block2 = classes * width
    volume = float(span * taps)

    chan = lax.axis_index("chan")
    tmpl = lax.axis_index("tmpl")
    core = chan % 2
    place_z = (chan // 2) % run
    place_y = chan // (2 * run)
    my_class = place_y * 2 + core
    x_count = tmpl_count // 2
    partner = tmpl + 1 - 2 * (tmpl % 2)
    sibling = chan + 1 - 2 * core

    def chan_of(cls, z):
        return ((cls // 2) * run + z) * 2 + cls % 2

    def x_peer(step):
        return (tmpl + 2 * step) % tmpl_count

    behind = ((chan - 2 + chan_count) % chan_count, tmpl)
    ahead = ((chan + 2) % chan_count, tmpl)
    before = (chan, (tmpl - 1 + tmpl_count) % tmpl_count)
    after = (chan, (tmpl + 1) % tmpl_count)

    barrier = pltpu.get_barrier_semaphore()
    greeted = [(chan_of((my_class + d) % classes, place_z), tmpl) for d in range(1, classes)]
    greeted += [(chan_of(my_class, (place_z + d) % run), tmpl) for d in range(1, run)]
    greeted += [(chan, x_peer(d)) for d in range(1, x_count)]
    greeted += [(chan, partner), behind, ahead, before, after]
    for device in greeted:
        pl.semaphore_signal(barrier, inc=1, device_id=device, device_id_type=MESH)

    bank[tmpl, 0:span, :] = tmpl_ref[...]
    bank[tmpl, span:, :] = jnp.full((bank.shape[1] - span, taps), off_ref[0, 0].astype(F32)).astype(BF16)

    out_row = iota((rows, rows), 0)
    in_row = iota((rows, rows), 1)
    ids = ids_ref[...]
    cls = out_row >> log2(block1)
    dest_z = (out_row >> log2(width)) & (run - 1)
    dest = (((cls >> 1) * run + dest_z) << 1) + (cls & 1)
    same = (in_row & (width - 1)) == (out_row & (width - 1))
    select = ((ids >> log2(per_group)) == dest) & same
    places = jnp.sum(jnp.where(select, (ids & (per_group - 1)) + 1, 0).astype(F32), axis=1, keepdims=True)
    snd1[:, 0:segment] = jnp.dot(
        select.astype(F32).astype(BF16), raw_ref[...], preferred_element_type=F32
    ).astype(BF16)
    snd1[:, segment:] = jnp.broadcast_to(places, (rows, LANES)).astype(BF16)

    pl.semaphore_wait(barrier, len(greeted))

    sends = []

    def send(src, dst, s_sem, r_sem, device):
        copy = pltpu.make_async_remote_copy(
            src_ref=src, dst_ref=dst, send_sem=s_sem, recv_sem=r_sem, device_id=device, device_id_type=MESH
        )
        copy.start()
        sends.append(copy)
        return copy

    def block(index, size):
        return pl.ds(pl.multiple_of(index * size, size), size)

    first = []
    for d in range(1, classes):
        target = (my_class + d) % classes
        first.append(send(
            snd1.at[block(target, block1)], rcv1.at[block(my_class, block1)],
            s1.at[d], r1.at[d], (chan_of(target, place_z), tmpl),
        ))
    cuts = [span // chunks * part for part in range(chunks)] + [bank.shape[1]]
    to_partner = [
        send(bank.at[tmpl, cuts[p]:cuts[p + 1]], bank.at[tmpl, cuts[p]:cuts[p + 1]], sz.at[p], rz.at[p], (chan, partner))
        for p in range(chunks)
    ]
    to_peers = [
        send(bank.at[tmpl], bank.at[tmpl], st.at[d], rt.at[d], (chan, x_peer(d))) for d in range(1, x_count)
    ]
    rcv1[block(my_class, block1), :] = snd1[block(my_class, block1), :]

    pad = pad_rows - total_rows
    for s in range(FOLD):
        deep[s * pad_rows + total_rows:(s + 1) * pad_rows, :] = jnp.zeros((pad, columns), BF16)
    for s in range(2):
        squares[s * pad_rows + total_rows:(s + 1) * pad_rows, :] = jnp.zeros((pad, squares.shape[1]), BF16)

    for copy in first:
        copy.wait_recv()

    source = ((out_row >> log2(width)) & (classes - 1)) * block1 + (out_row >> log2(block2)) * width + (out_row & (width - 1))
    order = (in_row == source).astype(F32).astype(BF16)
    snd2[...] = jnp.dot(order, rcv1[...], preferred_element_type=F32).astype(BF16)
    second = []
    for d in range(1, run):
        target = (place_z + d) % run
        second.append(send(
            snd2.at[block(target, block2)], rcv2.at[block(place_z, block2)],
            s2.at[d], r2.at[d], (chan_of(my_class, target), tmpl),
        ))
    rcv2[block(place_z, block2), :] = snd2[block(place_z, block2), :]
    for copy in second:
        copy.wait_recv()
    arrived = rcv2[:, segment:segment + LANES].astype(F32)
    slot_row = iota((rows, LANES), 0)
    fiber_row = iota((rows, LANES), 1)
    pick = (arrived == ((fiber_row >> log2(width)) + 1).astype(F32)) & (
        (slot_row & (width - 1)) == (fiber_row & (width - 1))
    )
    pick = jnp.transpose(pick.astype(F32))[0:group_rows, :].astype(BF16)
    rec[0:group_rows, :] = jnp.dot(pick, rcv2[:, 0:segment], preferred_element_type=F32).astype(BF16)

    def prepare(index):
        template = bank[index, 0:span, :]
        offset = bank[index, span:span + 16, :].astype(F32)[0:1, 0:1].astype(I32)
        shape = (span, pad_rows)
        inside = chan + (iota(shape, 1) >> log2(group_rows)) < chan_count
        moved = ((iota(shape, 1) - iota(shape, 0)) == offset) & inside
        turned = lax.dot_general(
            template, moved.astype(F32).astype(BF16), (((0,), (0,)), ((), ())), preferred_element_type=F32
        ).astype(BF16)
        for s in range(FOLD):
            weights[block(index, lag), s * pad_rows:(s + 1) * pad_rows] = turned[s * lag:(s + 1) * lag, :]
        wide = template.astype(F32)
        norms[pl.ds(index, 1), :] = jnp.sum(wide * wide, axis=0, keepdims=True)
        lane = iota((1, pad_rows), 1)
        covered = (lane >= offset) & (lane < offset + span) & (chan + (lane >> log2(group_rows)) < chan_count)
        masks[pl.ds(index, 1), :] = covered.astype(F32)

    def group(index):
        return pl.ds(pl.multiple_of(index * group_rows, group_rows), group_rows)

    first_samples = send(rec.at[0:group_rows, 0:taps], fol.at[0:group_rows], sf, rf, before)
    relay, relay_fol, cross, cross_fol = [None], [None], [None], [None]

    def pass_on(step):
        relay.append(send(rec.at[group(2 * step - 2)], rec.at[group(2 * step)], sr.at[step], rr.at[step], behind))

    def pass_on_fol(step):
        relay_fol.append(send(fol.at[group(2 * step - 2)], fol.at[group(2 * step)], srf.at[step], rrf.at[step], behind))

    pass_on(1)
    prepare(tmpl)
    first_samples.wait_recv()
    pass_on_fol(1)
    forwards = []
    for step in range(1, links + 1):
        relay[step].wait_recv()
        if step < links:
            pass_on(step + 1)
        cross.append(send(
            rec.at[group(2 * (step - core))], rec.at[group(2 * step - 1)], sq.at[step], rq.at[step], (sibling, tmpl)
        ))
        relay_fol[step].wait_recv()
        if step < links:
            pass_on_fol(step + 1)
        cross_fol.append(send(
            fol.at[group(2 * (step - core))], fol.at[group(2 * step - 1)], sqf.at[step], rqf.at[step], (sibling, tmpl)
        ))
        for p in range(chunks * (step - 1) // links, chunks * step // links):
            to_partner[p].wait_recv()
            for d in range(1, x_count):
                forwards.append(send(
                    bank.at[partner, cuts[p]:cuts[p + 1]], bank.at[partner, cuts[p]:cuts[p + 1]],
                    sn.at[d, p], rn.at[d, p], (chan, x_peer(d)),
                ))
        if step < x_count:
            to_peers[step - 1].wait_recv()
            prepare((tmpl - 2 * step + tmpl_count) % tmpl_count)
    prepare(partner)
    for copy in cross[1:] + cross_fol[1:]:
        copy.wait_recv()

    last = tmpl == tmpl_count - 1

    def spread(index, carry):
        here = pl.ds(pl.multiple_of(index * group_rows, group_rows), group_rows)

        def below(s):
            return pl.ds(pl.multiple_of(index * group_rows + s * pad_rows, group_rows), group_rows)

        main = rec[here, :].astype(F32)
        tail = jnp.where(last, jnp.zeros((), F32), fol[here, :].astype(F32))
        whole = jnp.concatenate([main, tail], axis=1)
        narrow = whole.astype(BF16)
        turned = pltpu.roll(whole, whole.shape[1] - lag, 1).astype(BF16)
        for s in range(FOLD):
            side = turned if s * lag % LANES else narrow
            begin = (s * lag) // LANES * LANES
            deep[below(s), :] = side[:, begin:begin + columns]
        squared = whole * whole
        high = squared.astype(BF16)
        squares[below(0), :] = high
        squares[below(1), :] = (squared - high.astype(F32)).astype(BF16)
        return carry

    lax.fori_loop(0, reach + 1, spread, 0)

    for p in range(chunks):
        for d in range(1, x_count):
            forwards[p * (x_count - 1) + d - 1].wait_recv()
    for d in range(1, x_count):
        prepare((partner - 2 * d + tmpl_count) % tmpl_count)
    norm = jnp.sum(norms[...], axis=1, keepdims=True)

    mask = masks[...].astype(BF16)
    energy = jnp.dot(
        jnp.concatenate([mask, mask], axis=1), squares[...], preferred_element_type=F32
    )
    shift = 1
    while shift < taps:
        energy = energy + pltpu.roll(energy, energy.shape[1] - shift, 1)
        shift *= 2
    energy = energy[:, 0:segment]

    tile = 3 * LANES

    def multiply(index, carry):
        here = pl.ds(pl.multiple_of(index * tile, tile), tile)
        prod[:, here] = jnp.dot(weights[...], deep[:, here], preferred_element_type=F32)
        return carry

    lax.fori_loop(0, columns // tile, multiply, 0)

    def fold(index, carry):
        part = prod[pl.ds(pl.multiple_of(index * lag, lag), lag), :]
        half = lag // 2
        while half >= 8:
            part = part[0:half, :] + pltpu.roll(part[half:, :], columns - half, 1)
            half //= 2
        for t in range(columns // LANES):
            strips[t, pl.ds(pl.multiple_of(index * 8, 8), 8), :] = part[:, t * LANES:(t + 1) * LANES]
        return carry

    lax.fori_loop(0, homed, fold, 0)
    numer = jnp.zeros((homed, columns), F32)
    for a in range(8):
        strip = jnp.concatenate([strips[t, pl.ds(a, homed, stride=8), :] for t in range(columns // LANES)], axis=1)
        numer = numer + (strip if a == 0 else pltpu.roll(strip, columns - a, 1))
    out_ref[...] = numer[:, 0:segment] * jnp.sqrt(volume / (jnp.maximum(energy, volume) * norm))

    for copy in sends:
        copy.wait_send()


def body(run, raw_stretches, stretch_ids, templates, offsets):
    chan_count = lax.axis_size("chan")
    tmpl_count = lax.axis_size("tmpl")
    slots, width, segment = raw_stretches.shape
    span, taps = templates.shape[2:]
    per_group = chan_count // 2
    group_rows = per_group * width
    reach = span // group_rows
    links = reach // 2
    rows = slots * width
    total_rows = (reach + 1) * group_rows
    pad_rows = -(-total_rows // LANES) * LANES
    lag = taps // FOLD
    columns = -(-(segment + lag) // (3 * LANES)) * 3 * LANES
    classes = chan_count // run
    x_count = tmpl_count // 2
    chunks = 4
    homed = tmpl_count
    dma = pltpu.SemaphoreType.DMA
    vmem = pl.BlockSpec(memory_space=pltpu.VMEM)
    pairs = [dma((classes,))] * 2 + [dma((run,))] * 2 + [dma((x_count,))] * 2 + [dma((chunks,))] * 2 + [dma] * 2
    pairs += [dma((links + 1,))] * 4 + [dma((x_count, chunks))] * 2 + [dma((links + 1,))] * 4
    detection = pl.pallas_call(
        functools.partial(kernel, chan_count, tmpl_count, run, width, per_group, chunks),
        out_shape=jax.ShapeDtypeStruct((homed, segment), F32),
        in_specs=[vmem, vmem, vmem, pl.BlockSpec(memory_space=pltpu.SMEM)],
        out_specs=vmem,
        scratch_shapes=[
            pltpu.VMEM((rows, segment + LANES), BF16),
            pltpu.VMEM((rows, segment + LANES), BF16),
            pltpu.VMEM((rows, segment + LANES), BF16),
            pltpu.VMEM((rows, segment + LANES), BF16),
            pltpu.VMEM((total_rows, segment), BF16),
            pltpu.VMEM((total_rows, taps), BF16),
            pltpu.VMEM((homed, span + 16, taps), BF16),
            pltpu.VMEM((FOLD * pad_rows, columns), BF16),
            pltpu.VMEM((homed * lag, FOLD * pad_rows), BF16),
            pltpu.VMEM((2 * pad_rows, segment + taps), BF16),
            pltpu.VMEM((homed * lag, columns), F32),
            pltpu.VMEM((columns // LANES, homed * 8, LANES), F32),
            pltpu.VMEM((homed, taps), F32),
            pltpu.VMEM((homed, pad_rows), F32),
            *pairs,
        ],
        compiler_params=pltpu.CompilerParams(
            collective_id=0, has_side_effects=True, vmem_limit_bytes=48 * 1024 * 1024
        ),
    )(
        raw_stretches.reshape(rows, segment),
        jnp.repeat(stretch_ids, width).reshape(1, rows),
        templates.reshape(span, taps),
        offsets,
    )
    return detection.reshape(1, homed, segment)


def solution(mesh, run=8):
    placed = (P("chan", None, "tmpl"), P("chan"), P("chan", "tmpl", None, None), P("chan", "tmpl"))
    return jax.shard_map(
        functools.partial(body, run), mesh=mesh, in_specs=placed, out_specs=P("chan", None, "tmpl"), check_vma=False
    )
```

```python
import functools

import jax
import jax.numpy as jnp
from jax import lax
from jax.experimental import pallas as pl
from jax.experimental.pallas import tpu as pltpu
from jax.sharding import PartitionSpec as P

MESH = pl.DeviceIdType.MESH
F32 = jnp.float32
BF16 = jnp.bfloat16
I32 = jnp.int32
FOLD = 2
LANES = 128


def iota(shape, axis):
    return lax.broadcasted_iota(I32, shape, axis)


def log2(number):
    return number.bit_length() - 1


def kernel(
    chan_count, tmpl_count, run, width, per_group,
    raw_ref, ids_ref, tmpl_ref, off_ref, out_ref,
    snd1, rcv1, snd2, rcv2, rec, bank, weights, squares, prod, strips, norms, masks, given, taken,
    s1, r1, s2, r2, st, rt, sd, rd, su, ru, scd, rcd, scu, rcu, sfe, rfe, sfo, rfo, so, ro,
):
    rows, segment = raw_ref.shape
    span, taps = tmpl_ref.shape
    group_rows = per_group * width
    reach = span // group_rows
    links = reach // 2
    total_rows = (reach + 1) * group_rows
    columns = prod.shape[1]
    lag = taps // FOLD
    x_count = tmpl_count // 2
    classes = chan_count // run
    block1 = run * width
    block2 = classes * width
    cut = segment // 2
    volume = float(span * taps)

    chan = lax.axis_index("chan")
    tmpl = lax.axis_index("tmpl")
    core = chan % 2
    place_z = (chan // 2) % run
    place_y = chan // (2 * run)
    place_x = tmpl // 2
    half = tmpl % 2
    my_class = place_y * 2 + core
    ring = place_z + run * half
    sibling = chan + 1 - 2 * core

    def chan_of(cls, z):
        return ((cls // 2) * run + z) * 2 + cls % 2

    def half_at(place):
        return ((place + 4 * run) % (2 * run)) // run

    def x_peer(step):
        return (tmpl + 2 * step + tmpl_count) % tmpl_count

    def near(steps, move):
        return ((chan + 2 * steps + 2 * chan_count) % chan_count, place_x * 2 + half_at(ring + move))

    parents = (
        {
            ("D", 1): ("D", 0), ("D", 3): ("D", 0), ("U", 2): ("D", 0), ("D", 2): ("D", 1), ("D", 4): ("D", 3),
            ("U", 4): ("U", 2), ("U", 0): ("U", 2), ("U", 3): ("U", 2), ("U", 1): ("U", 2),
        },
        {
            ("D", 1): ("D", 0), ("D", 3): ("D", 0), ("U", 3): ("D", 0), ("D", 2): ("D", 1), ("D", 4): ("D", 3),
            ("U", 0): ("U", 3), ("U", 1): ("U", 3), ("U", 2): ("U", 3), ("U", 4): ("U", 3),
        },
    )

    def route(node, parent):
        return parent[1] - node[1], parent[1] - node[1] + (run if node[0] != parent[0] else 0)

    partner = (chan, tmpl + 1 - 2 * half)
    earlier, earlier_sibling = (chan, x_peer(-1)), (sibling, x_peer(-1))

    barrier = pltpu.get_barrier_semaphore()
    greeted = [(chan_of((my_class + d) % classes, place_z), tmpl) for d in range(1, classes)]
    greeted += [(chan_of(my_class, (place_z + d) % run), tmpl) for d in range(1, run)]
    greeted += [(chan, x_peer(d)) for d in range(1, x_count)]
    routes = {route(*link) for table in parents for link in table.items()}
    routes = sorted(routes | {(-steps, -move) for steps, move in routes})
    greeted += [near(steps, move) for steps, move in routes]
    greeted += [partner, earlier_sibling, (sibling, x_peer(1))]
    for device in greeted:
        pl.semaphore_signal(barrier, inc=1, device_id=device, device_id_type=MESH)

    bank[place_x, 0:span, :] = tmpl_ref[...]
    bank[place_x, span:, :] = jnp.full((bank.shape[1] - span, taps), off_ref[0, 0].astype(F32)).astype(BF16)

    out_row = iota((rows, rows), 0)
    in_row = iota((rows, rows), 1)
    ids = ids_ref[...]
    cls = out_row >> log2(block1)
    dest_z = (out_row >> log2(width)) & (run - 1)
    dest = (((cls >> 1) * run + dest_z) << 1) + (cls & 1)
    same = (in_row & (width - 1)) == (out_row & (width - 1))
    select = ((ids >> log2(per_group)) == dest) & same
    places = jnp.sum(jnp.where(select, (ids & (per_group - 1)) + 1, 0).astype(F32), axis=1, keepdims=True)
    snd1[:, LANES:] = jnp.dot(
        select.astype(F32).astype(BF16), raw_ref[...], preferred_element_type=F32
    ).astype(BF16)
    snd1[:, 0:LANES] = jnp.broadcast_to(places, (rows, LANES)).astype(BF16)

    pl.semaphore_wait(barrier, len(greeted))

    sends = []

    def copy_to(src, dst, s_sem, r_sem, device):
        return pltpu.make_async_remote_copy(
            src_ref=src, dst_ref=dst, send_sem=s_sem, recv_sem=r_sem, device_id=device, device_id_type=MESH
        )

    def send(*args):
        copy = copy_to(*args)
        copy.start()
        sends.append(copy)
        return copy

    def block(index, size):
        return pl.ds(pl.multiple_of(index * size, size), size)

    stretches = (pl.ds(0, LANES + cut), pl.ds(LANES + cut, segment - cut))
    first = [[], []]
    for h, lanes in enumerate(stretches):
        for d in range(1, classes):
            target = (my_class + d) % classes
            first[h].append(send(
                snd1.at[block(target, block1), lanes], rcv1.at[block(my_class, block1), lanes],
                s1.at[d, h], r1.at[d, h], (chan_of(target, place_z), tmpl),
            ))
    to_peers = [
        send(bank.at[place_x], bank.at[place_x], st.at[d], rt.at[d], (chan, x_peer(d))) for d in range(1, x_count)
    ]
    rcv1[block(my_class, block1), :] = snd1[block(my_class, block1), :]

    source = ((out_row >> log2(width)) & (classes - 1)) * block1 + (out_row >> log2(block2)) * width + (out_row & (width - 1))
    order = (in_row == source).astype(F32).astype(BF16)
    second = [[], []]
    for h, lanes in enumerate(stretches):
        for copy in first[h]:
            copy.wait_recv()
        snd2[:, lanes] = jnp.dot(order, rcv1[:, lanes], preferred_element_type=F32).astype(BF16)
        for d in range(1, run):
            target = (place_z + d) % run
            second[h].append(send(
                snd2.at[block(target, block2), lanes], rcv2.at[block(place_z, block2), lanes],
                s2.at[d, h], r2.at[d, h], (chan_of(my_class, target), tmpl),
            ))
    rcv2[block(place_z, block2), :] = snd2[block(place_z, block2), :]

    def prepare(index):
        template = bank[index, 0:span, :]
        offset = bank[index, span:span + 16, :].astype(F32)[0:1, 0:1].astype(I32)
        shape = (span, total_rows)
        inside = chan + (iota(shape, 1) >> log2(group_rows)) < chan_count
        moved = ((iota(shape, 1) - iota(shape, 0)) == offset) & inside
        turned = lax.dot_general(
            template, moved.astype(F32).astype(BF16), (((0,), (0,)), ((), ())), preferred_element_type=F32
        ).astype(BF16)
        for s in range(FOLD):
            weights[s, block(index, lag), :] = turned[s * lag:(s + 1) * lag, :]
        wide = template.astype(F32)
        norms[pl.ds(index, 1), :] = jnp.sum(wide * wide, axis=0, keepdims=True)
        lane = iota((1, total_rows), 1)
        covered = (lane >= offset) & (lane < offset + span) & (chan + (lane >> log2(group_rows)) < chan_count)
        masks[pl.ds(index, 1), :] = covered.astype(F32)

    def group(index):
        return pl.ds(pl.multiple_of(index * group_rows, group_rows), group_rows)

    whole_down = ((0, cut), (cut, segment - cut))
    arrivals = {}

    def lanes_of(which, p):
        return pl.ds(pl.multiple_of(which * segment + whole_down[p][0], LANES), whole_down[p][1])

    def which_of(kind, j):
        near_half = half_at(ring + j)
        return near_half if kind == "D" else 1 - near_half

    def pass_on(parent, p):
        for node in parents[p]:
            if parents[p][node] == parent:
                (kind, j), lanes = node, lanes_of(which_of(*parent), p)
                s_sem, r_sem = {"D": (sd, rd), "U": (su, ru)}[kind]
                arrivals[kind, j, p] = send(
                    rec.at[group(2 * parent[1]), lanes], rec.at[group(2 * j), lanes], s_sem.at[j, p], r_sem.at[j, p],
                    near(*route(node, parent)),
                )

    def cross(t, kind, p):
        j = t - core
        lanes = lanes_of(which_of(kind, j), p)
        s_sem, r_sem = {"D": (scd, rcd), "U": (scu, rcu)}[kind]
        return copy_to(
            rec.at[group(2 * j), lanes], rec.at[group(2 * t - 1), lanes], s_sem.at[t, p], r_sem.at[t, p],
            (sibling, tmpl),
        )

    tail = pl.ds(2 * segment, taps)

    def lend(j):
        return copy_to(rec.at[group(2 * j), 0:taps], rec.at[group(2 * j), tail], sfe.at[j], rfe.at[j], earlier)

    def lend_cross(t):
        return copy_to(
            rec.at[group(2 * (t - core)), 0:taps], rec.at[group(2 * t - 1), tail], sfo.at[t], rfo.at[t],
            earlier_sibling,
        )

    def share(j, kind, p):
        which = which_of(kind, j)
        t = j + core
        inner = 1 <= j < links
        if inner:
            cross(t, kind, p).start()
        else:
            @pl.when(core == (1 if j == 0 else 0))
            def _():
                cross(t, kind, p).start()

        if p == 0:
            @pl.when(which == 0)
            def _():
                lend(j).start()
                if inner:
                    lend_cross(t).start()

            if not inner:
                @pl.when((which == 0) & (core == (1 if j == 0 else 0)))
                def _():
                    lend_cross(t).start()

    last = place_x == x_count - 1

    def square(index, lanes):
        value = rec[group(index), lanes].astype(F32)
        squared = value * value
        high = squared.astype(BF16)
        squares[0, group(index), lanes] = high
        squares[1, group(index), lanes] = (squared - high.astype(F32)).astype(BF16)

    def square_tail(index):
        @pl.when(last)
        def _():
            rec[group(index), tail] = jnp.zeros((group_rows, taps), BF16)

        square(index, tail)

    def finish_odd(t, kind):
        for p in range(2):
            copy = cross(t, kind, p)
            copy.wait_recv()
            square(2 * t - 1, lanes_of(which_of(kind, t - 1 + core), p))

    def finish_lent(j):
        lend(j).wait_recv()
        square_tail(2 * j)
        if j > 0:
            lend_cross(j).wait_recv()
            square_tail(2 * j - 1)

    prepare(place_x)
    arrived_rows = iota((rows, LANES), 0)
    fiber_row = iota((rows, LANES), 1)
    same_channel = (arrived_rows & (width - 1)) == (fiber_row & (width - 1))
    wanted = ((fiber_row >> log2(width)) + 1).astype(F32)
    for h in range(2):
        for copy in second[h]:
            copy.wait_recv()
        if h == 0:
            pick = (rcv2[:, 0:LANES].astype(F32) == wanted) & same_channel
            pick = jnp.transpose(pick.astype(F32))[0:group_rows, :].astype(BF16)
        begin, size = whole_down[h]
        rec[0:group_rows, lanes_of(half, h)] = jnp.dot(
            pick, rcv2[:, LANES + begin:LANES + begin + size], preferred_element_type=F32
        ).astype(BF16)
        pass_on(("D", 0), h)
        share(0, "D", h)
        square(0, lanes_of(half, h))
        if h == 0:
            to_peers[0].wait_recv()
            prepare((place_x - 1 + x_count) % x_count)

    def came(kind, j, p):
        arrivals[kind, j, p].wait_recv()
        pass_on((kind, j), p)
        share(j, kind, p)
        square(2 * j, lanes_of(which_of(kind, j), p))

    due = (
        {
            ("D", 1): 3, ("D", 3): 6, ("D", 2): 7, ("D", 4): 10, ("U", 2): 12,
            ("U", 3): 17, ("U", 1): 18, ("U", 4): 19, ("U", 0): 20,
        },
        {
            ("D", 1): 9, ("D", 3): 11, ("D", 2): 14, ("D", 4): 15, ("U", 3): 18,
            ("U", 4): 23, ("U", 2): 24, ("U", 1): 25, ("U", 0): 26,
        },
    )
    events = sorted((due[p][node], *node, p) for p in range(2) for node in parents[p])
    for count, (_, kind, j, p) in enumerate(events):
        came(kind, j, p)
        if 1 <= count < x_count - 1:
            to_peers[count].wait_recv()
            prepare((place_x - 1 - count + x_count) % x_count)
        if (kind, j, p) == ("U", 3, 1):
            for t in range(1, links + 1):
                finish_odd(t, "D")
    for t in range(1, links + 1):
        finish_odd(t, "U")
    for j in range(links, -1, -1):
        finish_lent(j)

    norm = jnp.sum(norms[...], axis=1, keepdims=True)
    mask = masks[...].astype(BF16)
    tile = LANES * (1 if columns % (3 * LANES) else 3)

    def score(which):
        def multiply(index, carry):
            here = pl.ds(pl.multiple_of(index * tile, tile), tile)
            there = pl.ds(pl.multiple_of(which * segment + index * tile, LANES), tile)
            total = jnp.dot(weights[0], rec[:, there], preferred_element_type=F32)
            for s in range(1, FOLD):
                there = pl.ds(pl.multiple_of(which * segment + index * tile + s * lag, LANES), tile)
                total = total + jnp.dot(weights[s], rec[:, there], preferred_element_type=F32)
            prod[:, here] = total
            return carry

        lax.fori_loop(0, columns // tile, multiply, 0)
        there = pl.ds(pl.multiple_of(which * segment, LANES), segment + taps)
        energy = jnp.dot(mask, squares[0, :, there], preferred_element_type=F32)
        energy = energy + jnp.dot(mask, squares[1, :, there], preferred_element_type=F32)
        shift = 1
        while shift < taps:
            energy = energy + pltpu.roll(energy, energy.shape[1] - shift, 1)
            shift *= 2
        energy = energy[:, 0:segment]

        def fold(index, carry):
            part = prod[pl.ds(pl.multiple_of(index * lag, lag), lag), :]
            size = lag // 2
            while size >= 8:
                part = part[0:size, :] + pltpu.roll(part[size:, :], columns - size, 1)
                size //= 2
            for t in range(columns // LANES):
                strips[t, pl.ds(pl.multiple_of(index * 8, 8), 8), :] = part[:, t * LANES:(t + 1) * LANES]
            return carry

        lax.fori_loop(0, x_count, fold, 0)
        numer = jnp.zeros((x_count, columns), F32)
        for a in range(8):
            strip = jnp.concatenate(
                [strips[t, pl.ds(a, x_count, stride=8), :] for t in range(columns // LANES)], axis=1
            )
            numer = numer + (strip if a == 0 else pltpu.roll(strip, columns - a, 1))
        return numer[:, 0:segment] * jnp.sqrt(volume / (jnp.maximum(energy, volume) * norm))

    given[...] = score(1 - half)
    trade = send(given, taken, so, ro, partner)
    own = score(half)
    for x in range(x_count):
        out_ref[pl.ds(2 * x + half, 1), :] = own[x:x + 1, :]
    trade.wait_recv()
    for x in range(x_count):
        out_ref[pl.ds(2 * x + 1 - half, 1), :] = taken[x:x + 1, :]

    for copy in sends:
        copy.wait_send()
    for t in range(1, links + 1):
        for kind in ("D", "U"):
            for p in range(2):
                cross(t, kind, p).wait_send()
        lend_cross(t).wait_send()
    for j in range(links + 1):
        lend(j).wait_send()


def body(run, raw_stretches, stretch_ids, templates, offsets):
    chan_count = lax.axis_size("chan")
    tmpl_count = lax.axis_size("tmpl")
    slots, width, segment = raw_stretches.shape
    span, taps = templates.shape[2:]
    per_group = chan_count // 2
    group_rows = per_group * width
    reach = span // group_rows
    links = reach // 2
    rows = slots * width
    total_rows = (reach + 1) * group_rows
    lag = taps // FOLD
    columns = segment + lag
    classes = chan_count // run
    x_count = tmpl_count // 2
    homed = tmpl_count
    dma = pltpu.SemaphoreType.DMA
    vmem = pl.BlockSpec(memory_space=pltpu.VMEM)
    pairs = [dma((classes, 2))] * 2 + [dma((run, 2))] * 2 + [dma((x_count,))] * 2
    pairs += [dma((links + 1, 2))] * 8 + [dma((links + 1,))] * 4 + [dma] * 2
    detection = pl.pallas_call(
        functools.partial(kernel, chan_count, tmpl_count, run, width, per_group),
        out_shape=jax.ShapeDtypeStruct((homed, segment), F32),
        in_specs=[vmem, vmem, vmem, pl.BlockSpec(memory_space=pltpu.SMEM)],
        out_specs=vmem,
        scratch_shapes=[
            pltpu.VMEM((rows, segment + LANES), BF16),
            pltpu.VMEM((rows, segment + LANES), BF16),
            pltpu.VMEM((rows, segment + LANES), BF16),
            pltpu.VMEM((rows, segment + LANES), BF16),
            pltpu.VMEM((total_rows, 2 * segment + taps), BF16),
            pltpu.VMEM((x_count, span + 16, taps), BF16),
            pltpu.VMEM((FOLD, x_count * lag, total_rows), BF16),
            pltpu.VMEM((2, total_rows, 2 * segment + taps), BF16),
            pltpu.VMEM((x_count * lag, columns), F32),
            pltpu.VMEM((columns // LANES, x_count * 8, LANES), F32),
            pltpu.VMEM((x_count, taps), F32),
            pltpu.VMEM((x_count, total_rows), F32),
            pltpu.VMEM((x_count, segment), F32),
            pltpu.VMEM((x_count, segment), F32),
            *pairs,
        ],
        compiler_params=pltpu.CompilerParams(
            collective_id=0, has_side_effects=True, vmem_limit_bytes=48 * 1024 * 1024
        ),
    )(
        raw_stretches.reshape(rows, segment),
        jnp.repeat(stretch_ids, width).reshape(1, rows),
        templates.reshape(span, taps),
        offsets,
    )
    return detection.reshape(1, homed, segment)


def solution(mesh, run=8):
    placed = (P("chan", None, "tmpl"), P("chan"), P("chan", "tmpl", None, None), P("chan", "tmpl"))
    return jax.shard_map(
        functools.partial(body, run), mesh=mesh, in_specs=placed, out_specs=P("chan", None, "tmpl"), check_vma=False
    )
```

```python
import functools

import jax
import jax.numpy as jnp
from jax import lax
from jax.experimental import pallas as pl
from jax.experimental.pallas import tpu as pltpu
from jax.sharding import PartitionSpec as P

MESH = pl.DeviceIdType.MESH
F32 = jnp.float32
BF16 = jnp.bfloat16
I32 = jnp.int32
FOLD = 2
LANES = 128


def iota(shape, axis):
    return lax.broadcasted_iota(I32, shape, axis)


def log2(number):
    return number.bit_length() - 1


def kernel(
    chan_count, tmpl_count, run, width, per_group,
    raw_ref, ids_ref, tmpl_ref, off_ref, out_ref,
    snd1, rcv1, snd2, rcv2, rec, bank, weights, squares, prod, strips, norms, masks, given, taken,
    s1, r1, s2, r2, st, rt, sd, rd, su, ru, scd, rcd, scu, rcu, sfe, rfe, sfo, rfo, so, ro,
):
    rows, segment = raw_ref.shape
    span, taps = tmpl_ref.shape
    group_rows = per_group * width
    reach = span // group_rows
    links = reach // 2
    total_rows = (reach + 1) * group_rows
    columns = prod.shape[1]
    lag = taps // FOLD
    x_count = tmpl_count // 2
    classes = chan_count // run
    block1 = run * width
    block2 = classes * width
    cut = segment // 2
    volume = float(span * taps)

    chan = lax.axis_index("chan")
    tmpl = lax.axis_index("tmpl")
    core = chan % 2
    place_z = (chan // 2) % run
    place_y = chan // (2 * run)
    place_x = tmpl // 2
    half = tmpl % 2
    my_class = place_y * 2 + core
    ring = place_z + run * half
    sibling = chan + 1 - 2 * core

    def chan_of(cls, z):
        return ((cls // 2) * run + z) * 2 + cls % 2

    def half_at(place):
        return ((place + 4 * run) % (2 * run)) // run

    def x_peer(step):
        return (tmpl + 2 * step + tmpl_count) % tmpl_count

    def near(steps, move):
        return ((chan + 2 * steps + 2 * chan_count) % chan_count, place_x * 2 + half_at(ring + move))

    parents = (
        {
            ("D", 1): ("D", 0), ("D", 2): ("D", 0), ("D", 3): ("D", 2), ("D", 4): ("D", 2), ("U", 2): ("D", 0),
            ("U", 1): ("U", 2), ("U", 3): ("U", 2), ("U", 0): ("U", 1), ("U", 4): ("U", 3),
        },
        {
            ("D", 1): ("D", 0), ("D", 2): ("D", 0), ("D", 3): ("D", 2), ("D", 4): ("D", 2), ("U", 2): ("D", 0),
            ("U", 4): ("U", 2), ("U", 0): ("U", 2), ("U", 3): ("U", 2), ("U", 1): ("U", 2),
        },
    )

    def route(node, parent):
        return parent[1] - node[1], parent[1] - node[1] + (run if node[0] != parent[0] else 0)

    partner = (chan, tmpl + 1 - 2 * half)
    earlier, earlier_sibling = (chan, x_peer(-1)), (sibling, x_peer(-1))

    barrier = pltpu.get_barrier_semaphore()
    greeted = [(chan_of((my_class + d) % classes, place_z), tmpl) for d in range(1, classes)]
    greeted += [(chan_of(my_class, (place_z + d) % run), tmpl) for d in range(1, run)]
    greeted += [(chan, x_peer(d)) for d in range(1, x_count)]
    routes = {route(*link) for table in parents for link in table.items()}
    routes = sorted(routes | {(-steps, -move) for steps, move in routes})
    greeted += [near(steps, move) for steps, move in routes]
    greeted += [partner, earlier_sibling, (sibling, x_peer(1))]
    for device in greeted:
        pl.semaphore_signal(barrier, inc=1, device_id=device, device_id_type=MESH)

    bank[place_x, 0:span, :] = tmpl_ref[...]
    bank[place_x, span:, :] = jnp.full((bank.shape[1] - span, taps), off_ref[0, 0].astype(F32)).astype(BF16)

    out_row = iota((rows, rows), 0)
    in_row = iota((rows, rows), 1)
    ids = ids_ref[...]
    cls = out_row >> log2(block1)
    dest_z = (out_row >> log2(width)) & (run - 1)
    dest = (((cls >> 1) * run + dest_z) << 1) + (cls & 1)
    same = (in_row & (width - 1)) == (out_row & (width - 1))
    select = ((ids >> log2(per_group)) == dest) & same
    places = jnp.sum(jnp.where(select, (ids & (per_group - 1)) + 1, 0).astype(F32), axis=1, keepdims=True)
    snd1[:, LANES:] = jnp.dot(
        select.astype(F32).astype(BF16), raw_ref[...], preferred_element_type=F32
    ).astype(BF16)
    snd1[:, 0:LANES] = jnp.broadcast_to(places, (rows, LANES)).astype(BF16)

    pl.semaphore_wait(barrier, len(greeted))

    sends = []

    def copy_to(src, dst, s_sem, r_sem, device):
        return pltpu.make_async_remote_copy(
            src_ref=src, dst_ref=dst, send_sem=s_sem, recv_sem=r_sem, device_id=device, device_id_type=MESH
        )

    def send(*args):
        copy = copy_to(*args)
        copy.start()
        sends.append(copy)
        return copy

    def block(index, size):
        return pl.ds(pl.multiple_of(index * size, size), size)

    stretches = (pl.ds(0, LANES + cut), pl.ds(LANES + cut, segment - cut))
    first = [[], []]
    for h, lanes in enumerate(stretches):
        for d in range(1, classes):
            target = (my_class + d) % classes
            first[h].append(send(
                snd1.at[block(target, block1), lanes], rcv1.at[block(my_class, block1), lanes],
                s1.at[d, h], r1.at[d, h], (chan_of(target, place_z), tmpl),
            ))
    to_peers = [
        send(bank.at[place_x], bank.at[place_x], st.at[d], rt.at[d], (chan, x_peer(d))) for d in range(1, x_count)
    ]
    rcv1[block(my_class, block1), :] = snd1[block(my_class, block1), :]

    source = ((out_row >> log2(width)) & (classes - 1)) * block1 + (out_row >> log2(block2)) * width + (out_row & (width - 1))
    order = (in_row == source).astype(F32).astype(BF16)
    second = [[], []]
    for h, lanes in enumerate(stretches):
        for copy in first[h]:
            copy.wait_recv()
        snd2[:, lanes] = jnp.dot(order, rcv1[:, lanes], preferred_element_type=F32).astype(BF16)
        for d in range(1, run):
            target = (place_z + d) % run
            second[h].append(send(
                snd2.at[block(target, block2), lanes], rcv2.at[block(place_z, block2), lanes],
                s2.at[d, h], r2.at[d, h], (chan_of(my_class, target), tmpl),
            ))
    rcv2[block(place_z, block2), :] = snd2[block(place_z, block2), :]

    def prepare(index):
        template = bank[index, 0:span, :]
        offset = bank[index, span:span + 16, :].astype(F32)[0:1, 0:1].astype(I32)
        shape = (span, total_rows)
        inside = chan + (iota(shape, 1) >> log2(group_rows)) < chan_count
        moved = ((iota(shape, 1) - iota(shape, 0)) == offset) & inside
        turned = lax.dot_general(
            template, moved.astype(F32).astype(BF16), (((0,), (0,)), ((), ())), preferred_element_type=F32
        ).astype(BF16)
        for s in range(FOLD):
            weights[s, block(index, lag), :] = turned[s * lag:(s + 1) * lag, :]
        wide = template.astype(F32)
        norms[pl.ds(index, 1), :] = jnp.sum(wide * wide, axis=0, keepdims=True)
        lane = iota((1, total_rows), 1)
        covered = (lane >= offset) & (lane < offset + span) & (chan + (lane >> log2(group_rows)) < chan_count)
        masks[pl.ds(index, 1), :] = covered.astype(F32)

    def group(index):
        return pl.ds(pl.multiple_of(index * group_rows, group_rows), group_rows)

    whole_down = ((0, cut), (cut, segment - cut))
    arrivals = {}

    def lanes_of(which, p):
        return pl.ds(pl.multiple_of(which * segment + whole_down[p][0], LANES), whole_down[p][1])

    def which_of(kind, j):
        near_half = half_at(ring + j)
        return near_half if kind == "D" else 1 - near_half

    def pass_on(parent, p):
        for node in parents[p]:
            if parents[p][node] == parent:
                (kind, j), lanes = node, lanes_of(which_of(*parent), p)
                s_sem, r_sem = {"D": (sd, rd), "U": (su, ru)}[kind]
                arrivals[kind, j, p] = send(
                    rec.at[group(2 * parent[1]), lanes], rec.at[group(2 * j), lanes], s_sem.at[j, p], r_sem.at[j, p],
                    near(*route(node, parent)),
                )

    def cross(t, kind, p):
        j = t - core
        lanes = lanes_of(which_of(kind, j), p)
        s_sem, r_sem = {"D": (scd, rcd), "U": (scu, rcu)}[kind]
        return copy_to(
            rec.at[group(2 * j), lanes], rec.at[group(2 * t - 1), lanes], s_sem.at[t, p], r_sem.at[t, p],
            (sibling, tmpl),
        )

    tail = pl.ds(2 * segment, taps)

    def lend(j):
        return copy_to(rec.at[group(2 * j), 0:taps], rec.at[group(2 * j), tail], sfe.at[j], rfe.at[j], earlier)

    def lend_cross(t):
        return copy_to(
            rec.at[group(2 * (t - core)), 0:taps], rec.at[group(2 * t - 1), tail], sfo.at[t], rfo.at[t],
            earlier_sibling,
        )

    def share(j, kind, p):
        which = which_of(kind, j)
        t = j + core
        inner = 1 <= j < links
        if inner:
            cross(t, kind, p).start()
        else:
            @pl.when(core == (1 if j == 0 else 0))
            def _():
                cross(t, kind, p).start()

        if p == 0:
            @pl.when(which == 0)
            def _():
                lend(j).start()
                if inner:
                    lend_cross(t).start()

            if not inner:
                @pl.when((which == 0) & (core == (1 if j == 0 else 0)))
                def _():
                    lend_cross(t).start()

    last = place_x == x_count - 1

    def square(index, lanes):
        value = rec[group(index), lanes].astype(F32)
        squared = value * value
        high = squared.astype(BF16)
        squares[0, group(index), lanes] = high
        squares[1, group(index), lanes] = (squared - high.astype(F32)).astype(BF16)

    def square_tail(index):
        @pl.when(last)
        def _():
            rec[group(index), tail] = jnp.zeros((group_rows, taps), BF16)

        square(index, tail)

    def finish_odd(t, kind):
        for p in range(2):
            copy = cross(t, kind, p)
            copy.wait_recv()
            square(2 * t - 1, lanes_of(which_of(kind, t - 1 + core), p))

    def finish_lent(j):
        lend(j).wait_recv()
        square_tail(2 * j)
        if j > 0:
            lend_cross(j).wait_recv()
            square_tail(2 * j - 1)

    prepare(place_x)
    arrived_rows = iota((rows, LANES), 0)
    fiber_row = iota((rows, LANES), 1)
    same_channel = (arrived_rows & (width - 1)) == (fiber_row & (width - 1))
    wanted = ((fiber_row >> log2(width)) + 1).astype(F32)
    for h in range(2):
        for copy in second[h]:
            copy.wait_recv()
        if h == 0:
            pick = (rcv2[:, 0:LANES].astype(F32) == wanted) & same_channel
            pick = jnp.transpose(pick.astype(F32))[0:group_rows, :].astype(BF16)
        begin, size = whole_down[h]
        rec[0:group_rows, lanes_of(half, h)] = jnp.dot(
            pick, rcv2[:, LANES + begin:LANES + begin + size], preferred_element_type=F32
        ).astype(BF16)
        pass_on(("D", 0), h)
        share(0, "D", h)
        square(0, lanes_of(half, h))
        if h == 0:
            to_peers[0].wait_recv()
            prepare((place_x - 1 + x_count) % x_count)

    def came(kind, j, p):
        arrivals[kind, j, p].wait_recv()
        pass_on((kind, j), p)
        share(j, kind, p)
        square(2 * j, lanes_of(which_of(kind, j), p))

    due = (
        {
            ("D", 1): 4, ("D", 2): 5, ("D", 3): 10, ("D", 4): 11, ("U", 2): 10,
            ("U", 1): 14, ("U", 3): 15, ("U", 0): 18, ("U", 4): 19,
        },
        {
            ("D", 1): 11, ("D", 2): 12, ("D", 3): 16, ("D", 4): 17, ("U", 2): 17,
            ("U", 1): 21, ("U", 3): 22, ("U", 0): 23, ("U", 4): 24,
        },
    )
    events = sorted((due[p][node], *node, p) for p in range(2) for node in parents[p])
    for count, (_, kind, j, p) in enumerate(events):
        came(kind, j, p)
        if 1 <= count < x_count - 1:
            to_peers[count].wait_recv()
            prepare((place_x - 1 - count + x_count) % x_count)
        if (kind, j, p) == ("D", links, 1):
            for t in range(1, links + 1):
                finish_odd(t, "D")
    for t in range(1, links + 1):
        finish_odd(t, "U")
    for j in range(links, -1, -1):
        finish_lent(j)

    norm = jnp.sum(norms[...], axis=1, keepdims=True)
    mask = masks[...].astype(BF16)
    tile = LANES * (1 if columns % (3 * LANES) else 3)

    def score(which):
        def multiply(index, carry):
            here = pl.ds(pl.multiple_of(index * tile, tile), tile)
            there = pl.ds(pl.multiple_of(which * segment + index * tile, LANES), tile)
            total = jnp.dot(weights[0], rec[:, there], preferred_element_type=F32)
            for s in range(1, FOLD):
                there = pl.ds(pl.multiple_of(which * segment + index * tile + s * lag, LANES), tile)
                total = total + jnp.dot(weights[s], rec[:, there], preferred_element_type=F32)
            prod[:, here] = total
            return carry

        lax.fori_loop(0, columns // tile, multiply, 0)
        there = pl.ds(pl.multiple_of(which * segment, LANES), segment + taps)
        energy = jnp.dot(mask, squares[0, :, there], preferred_element_type=F32)
        energy = energy + jnp.dot(mask, squares[1, :, there], preferred_element_type=F32)
        shift = 1
        while shift < taps:
            energy = energy + pltpu.roll(energy, energy.shape[1] - shift, 1)
            shift *= 2
        energy = energy[:, 0:segment]

        def fold(index, carry):
            part = prod[pl.ds(pl.multiple_of(index * lag, lag), lag), :]
            size = lag // 2
            while size >= 8:
                part = part[0:size, :] + pltpu.roll(part[size:, :], columns - size, 1)
                size //= 2
            for t in range(columns // LANES):
                strips[t, pl.ds(pl.multiple_of(index * 8, 8), 8), :] = part[:, t * LANES:(t + 1) * LANES]
            return carry

        lax.fori_loop(0, x_count, fold, 0)
        numer = jnp.zeros((x_count, columns), F32)
        for a in range(8):
            strip = jnp.concatenate(
                [strips[t, pl.ds(a, x_count, stride=8), :] for t in range(columns // LANES)], axis=1
            )
            numer = numer + (strip if a == 0 else pltpu.roll(strip, columns - a, 1))
        return numer[:, 0:segment] * jnp.sqrt(volume / (jnp.maximum(energy, volume) * norm))

    given[...] = score(1 - half)
    trade = send(given, taken, so, ro, partner)
    own = score(half)
    for x in range(x_count):
        out_ref[pl.ds(2 * x + half, 1), :] = own[x:x + 1, :]
    trade.wait_recv()
    for x in range(x_count):
        out_ref[pl.ds(2 * x + 1 - half, 1), :] = taken[x:x + 1, :]

    for copy in sends:
        copy.wait_send()
    for t in range(1, links + 1):
        for kind in ("D", "U"):
            for p in range(2):
                cross(t, kind, p).wait_send()
        lend_cross(t).wait_send()
    for j in range(links + 1):
        lend(j).wait_send()


def body(run, raw_stretches, stretch_ids, templates, offsets):
    chan_count = lax.axis_size("chan")
    tmpl_count = lax.axis_size("tmpl")
    slots, width, segment = raw_stretches.shape
    span, taps = templates.shape[2:]
    per_group = chan_count // 2
    group_rows = per_group * width
    reach = span // group_rows
    links = reach // 2
    rows = slots * width
    total_rows = (reach + 1) * group_rows
    lag = taps // FOLD
    columns = segment + lag
    classes = chan_count // run
    x_count = tmpl_count // 2
    homed = tmpl_count
    dma = pltpu.SemaphoreType.DMA
    vmem = pl.BlockSpec(memory_space=pltpu.VMEM)
    pairs = [dma((classes, 2))] * 2 + [dma((run, 2))] * 2 + [dma((x_count,))] * 2
    pairs += [dma((links + 1, 2))] * 8 + [dma((links + 1,))] * 4 + [dma] * 2
    detection = pl.pallas_call(
        functools.partial(kernel, chan_count, tmpl_count, run, width, per_group),
        out_shape=jax.ShapeDtypeStruct((homed, segment), F32),
        in_specs=[vmem, vmem, vmem, pl.BlockSpec(memory_space=pltpu.SMEM)],
        out_specs=vmem,
        scratch_shapes=[
            pltpu.VMEM((rows, segment + LANES), BF16),
            pltpu.VMEM((rows, segment + LANES), BF16),
            pltpu.VMEM((rows, segment + LANES), BF16),
            pltpu.VMEM((rows, segment + LANES), BF16),
            pltpu.VMEM((total_rows, 2 * segment + taps), BF16),
            pltpu.VMEM((x_count, span + 16, taps), BF16),
            pltpu.VMEM((FOLD, x_count * lag, total_rows), BF16),
            pltpu.VMEM((2, total_rows, 2 * segment + taps), BF16),
            pltpu.VMEM((x_count * lag, columns), F32),
            pltpu.VMEM((columns // LANES, x_count * 8, LANES), F32),
            pltpu.VMEM((x_count, taps), F32),
            pltpu.VMEM((x_count, total_rows), F32),
            pltpu.VMEM((x_count, segment), F32),
            pltpu.VMEM((x_count, segment), F32),
            *pairs,
        ],
        compiler_params=pltpu.CompilerParams(
            collective_id=0, has_side_effects=True, vmem_limit_bytes=48 * 1024 * 1024
        ),
    )(
        raw_stretches.reshape(rows, segment),
        jnp.repeat(stretch_ids, width).reshape(1, rows),
        templates.reshape(span, taps),
        offsets,
    )
    return detection.reshape(1, homed, segment)


def solution(mesh, run=8):
    placed = (P("chan", None, "tmpl"), P("chan"), P("chan", "tmpl", None, None), P("chan", "tmpl"))
    return jax.shard_map(
        functools.partial(body, run), mesh=mesh, in_specs=placed, out_specs=P("chan", None, "tmpl"), check_vma=False
    )
```

```python
import functools

import jax
import jax.numpy as jnp
from jax import lax
from jax.experimental import pallas as pl
from jax.experimental.pallas import tpu as pltpu
from jax.sharding import PartitionSpec as P

MESH = pl.DeviceIdType.MESH
F32 = jnp.float32
BF16 = jnp.bfloat16
I32 = jnp.int32
FOLD = 2
LANES = 128


def iota(shape, axis):
    return lax.broadcasted_iota(I32, shape, axis)


def log2(number):
    return number.bit_length() - 1


def kernel(
    chan_count, tmpl_count, run, width, per_group,
    raw_ref, ids_ref, tmpl_ref, off_ref, out_ref,
    snd1, rcv1, snd2, rcv2, rec, bank, weights, squares, prod, strips, norms, masks, given, taken,
    s1, r1, s2, r2, st, rt, sd, rd, su, ru, scd, rcd, scu, rcu, sfe, rfe, sfo, rfo, so, ro,
):
    rows, segment = raw_ref.shape
    span, taps = tmpl_ref.shape
    group_rows = per_group * width
    reach = span // group_rows
    links = reach // 2
    total_rows = (reach + 1) * group_rows
    columns = prod.shape[1]
    lag = taps // FOLD
    x_count = tmpl_count // 2
    classes = chan_count // run
    block1 = run * width
    block2 = classes * width
    cut = segment // 2
    volume = float(span * taps)

    chan = lax.axis_index("chan")
    tmpl = lax.axis_index("tmpl")
    core = chan % 2
    place_z = (chan // 2) % run
    place_y = chan // (2 * run)
    place_x = tmpl // 2
    half = tmpl % 2
    my_class = place_y * 2 + core
    ring = place_z + run * half
    sibling = chan + 1 - 2 * core

    def chan_of(cls, z):
        return ((cls // 2) * run + z) * 2 + cls % 2

    def half_at(place):
        return ((place + 4 * run) % (2 * run)) // run

    def x_peer(step):
        return (tmpl + 2 * step + tmpl_count) % tmpl_count

    def near(steps, move):
        return ((chan + 2 * steps + 2 * chan_count) % chan_count, place_x * 2 + half_at(ring + move))

    parents = (
        {
            ("D", 1): ("D", 0), ("D", 2): ("D", 0), ("D", 3): ("D", 2), ("D", 4): ("D", 2), ("U", 2): ("D", 0),
            ("U", 1): ("U", 2), ("U", 3): ("U", 2), ("U", 0): ("U", 1), ("U", 4): ("U", 3),
        },
        {
            ("D", 1): ("D", 0), ("D", 2): ("D", 0), ("D", 3): ("D", 2), ("D", 4): ("D", 2), ("U", 2): ("D", 0),
            ("U", 4): ("U", 2), ("U", 0): ("U", 2), ("U", 3): ("U", 2), ("U", 1): ("U", 2),
        },
    )

    def route(node, parent):
        return parent[1] - node[1], parent[1] - node[1] + (run if node[0] != parent[0] else 0)

    partner = (chan, tmpl + 1 - 2 * half)
    earlier, earlier_sibling = (chan, x_peer(-1)), (sibling, x_peer(-1))

    barrier = pltpu.get_barrier_semaphore()
    greeted = [(chan_of((my_class + d) % classes, place_z), tmpl) for d in range(1, classes)]
    greeted += [(chan_of(my_class, (place_z + d) % run), tmpl) for d in range(1, run)]
    greeted += [(chan, x_peer(d)) for d in range(1, x_count)]
    routes = {route(*link) for table in parents for link in table.items()}
    routes = sorted(routes | {(-steps, -move) for steps, move in routes})
    greeted += [near(steps, move) for steps, move in routes]
    greeted += [partner, earlier_sibling, (sibling, x_peer(1))]
    for device in greeted:
        pl.semaphore_signal(barrier, inc=1, device_id=device, device_id_type=MESH)

    bank[place_x, 0:span, :] = tmpl_ref[...]
    bank[place_x, span:, :] = jnp.full((bank.shape[1] - span, taps), off_ref[0, 0].astype(F32)).astype(BF16)

    out_row = iota((rows, rows), 0)
    in_row = iota((rows, rows), 1)
    slots = rows // width
    ids = jnp.broadcast_to(ids_ref[...], (8, slots))
    parts = jnp.where(iota((8, slots), 0) == 0, ids >> log2(per_group), ids & (per_group - 1))
    spread = iota((slots, rows), 0) == (iota((slots, rows), 1) >> log2(width))
    parts = jnp.dot(
        parts.astype(F32).astype(BF16), spread.astype(F32).astype(BF16), preferred_element_type=F32
    ).astype(I32)
    cls = out_row >> log2(block1)
    dest_z = (out_row >> log2(width)) & (run - 1)
    dest = (((cls >> 1) * run + dest_z) << 1) + (cls & 1)
    same = (in_row & (width - 1)) == (out_row & (width - 1))
    select = (parts[0:1, :] == dest) & same
    places = jnp.sum(jnp.where(select, parts[1:2, :] + 1, 0).astype(F32), axis=1, keepdims=True)
    snd1[:, LANES:] = jnp.dot(
        select.astype(F32).astype(BF16), raw_ref[...], preferred_element_type=F32
    ).astype(BF16)
    snd1[:, 0:LANES] = jnp.broadcast_to(places, (rows, LANES)).astype(BF16)

    pl.semaphore_wait(barrier, len(greeted))

    sends = []

    def copy_to(src, dst, s_sem, r_sem, device):
        return pltpu.make_async_remote_copy(
            src_ref=src, dst_ref=dst, send_sem=s_sem, recv_sem=r_sem, device_id=device, device_id_type=MESH
        )

    def send(*args):
        copy = copy_to(*args)
        copy.start()
        sends.append(copy)
        return copy

    def block(index, size):
        return pl.ds(pl.multiple_of(index * size, size), size)

    stretches = (pl.ds(0, LANES + cut), pl.ds(LANES + cut, segment - cut))
    first = [[], []]
    for h, lanes in enumerate(stretches):
        for d in range(1, classes):
            target = (my_class + d) % classes
            first[h].append(send(
                snd1.at[block(target, block1), lanes], rcv1.at[block(my_class, block1), lanes],
                s1.at[d, h], r1.at[d, h], (chan_of(target, place_z), tmpl),
            ))
    to_peers = [
        send(bank.at[place_x], bank.at[place_x], st.at[d], rt.at[d], (chan, x_peer(d))) for d in range(1, x_count)
    ]
    rcv1[block(my_class, block1), :] = snd1[block(my_class, block1), :]

    source = ((out_row >> log2(width)) & (classes - 1)) * block1 + (out_row >> log2(block2)) * width + (out_row & (width - 1))
    order = (in_row == source).astype(F32).astype(BF16)
    second = [[], []]
    for h, lanes in enumerate(stretches):
        for copy in first[h]:
            copy.wait_recv()
        snd2[:, lanes] = jnp.dot(order, rcv1[:, lanes], preferred_element_type=F32).astype(BF16)
        for d in range(1, run):
            target = (place_z + d) % run
            second[h].append(send(
                snd2.at[block(target, block2), lanes], rcv2.at[block(place_z, block2), lanes],
                s2.at[d, h], r2.at[d, h], (chan_of(my_class, target), tmpl),
            ))
    rcv2[block(place_z, block2), :] = snd2[block(place_z, block2), :]

    def prepare(index):
        template = bank[index, 0:span, :]
        offset = bank[index, span:span + 16, :].astype(F32)[0:1, 0:1].astype(I32)
        shape = (span, total_rows)
        inside = chan + (iota(shape, 1) >> log2(group_rows)) < chan_count
        moved = ((iota(shape, 1) - iota(shape, 0)) == offset) & inside
        turned = lax.dot_general(
            template, moved.astype(F32).astype(BF16), (((0,), (0,)), ((), ())), preferred_element_type=F32
        ).astype(BF16)
        for s in range(FOLD):
            weights[s, block(index, lag), :] = turned[s * lag:(s + 1) * lag, :]
        wide = template.astype(F32)
        norms[pl.ds(index, 1), :] = jnp.sum(wide * wide, axis=0, keepdims=True)
        lane = iota((1, total_rows), 1)
        covered = (lane >= offset) & (lane < offset + span) & (chan + (lane >> log2(group_rows)) < chan_count)
        masks[pl.ds(index, 1), :] = covered.astype(F32)

    def group(index):
        return pl.ds(pl.multiple_of(index * group_rows, group_rows), group_rows)

    whole_down = ((0, cut), (cut, segment - cut))
    arrivals = {}

    def lanes_of(which, p):
        return pl.ds(pl.multiple_of(which * segment + whole_down[p][0], LANES), whole_down[p][1])

    def which_of(kind, j):
        near_half = half_at(ring + j)
        return near_half if kind == "D" else 1 - near_half

    def pass_on(parent, p):
        for node in parents[p]:
            if parents[p][node] == parent:
                (kind, j), lanes = node, lanes_of(which_of(*parent), p)
                s_sem, r_sem = {"D": (sd, rd), "U": (su, ru)}[kind]
                arrivals[kind, j, p] = send(
                    rec.at[group(2 * parent[1]), lanes], rec.at[group(2 * j), lanes], s_sem.at[j, p], r_sem.at[j, p],
                    near(*route(node, parent)),
                )

    def cross(t, kind, p):
        j = t - core
        lanes = lanes_of(which_of(kind, j), p)
        s_sem, r_sem = {"D": (scd, rcd), "U": (scu, rcu)}[kind]
        return copy_to(
            rec.at[group(2 * j), lanes], rec.at[group(2 * t - 1), lanes], s_sem.at[t, p], r_sem.at[t, p],
            (sibling, tmpl),
        )

    tail = pl.ds(2 * segment, taps)

    def lend(j):
        return copy_to(rec.at[group(2 * j), 0:taps], rec.at[group(2 * j), tail], sfe.at[j], rfe.at[j], earlier)

    def lend_cross(t):
        return copy_to(
            rec.at[group(2 * (t - core)), 0:taps], rec.at[group(2 * t - 1), tail], sfo.at[t], rfo.at[t],
            earlier_sibling,
        )

    def share(j, kind, p):
        which = which_of(kind, j)
        t = j + core
        inner = 1 <= j < links
        if inner:
            cross(t, kind, p).start()
        else:
            @pl.when(core == (1 if j == 0 else 0))
            def _():
                cross(t, kind, p).start()

        if p == 0:
            @pl.when(which == 0)
            def _():
                lend(j).start()
                if inner:
                    lend_cross(t).start()

            if not inner:
                @pl.when((which == 0) & (core == (1 if j == 0 else 0)))
                def _():
                    lend_cross(t).start()

    last = place_x == x_count - 1

    def square(index, lanes):
        value = rec[group(index), lanes].astype(F32)
        squared = value * value
        high = squared.astype(BF16)
        squares[0, group(index), lanes] = high
        squares[1, group(index), lanes] = (squared - high.astype(F32)).astype(BF16)

    def square_tail(index):
        @pl.when(last)
        def _():
            rec[group(index), tail] = jnp.zeros((group_rows, taps), BF16)

        square(index, tail)

    def finish_odd(t, kind):
        for p in range(2):
            copy = cross(t, kind, p)
            copy.wait_recv()
            square(2 * t - 1, lanes_of(which_of(kind, t - 1 + core), p))

    def finish_lent(j):
        lend(j).wait_recv()
        square_tail(2 * j)
        if j > 0:
            lend_cross(j).wait_recv()
            square_tail(2 * j - 1)

    prepare(place_x)
    arrived_rows = iota((rows, LANES), 0)
    fiber_row = iota((rows, LANES), 1)
    same_channel = (arrived_rows & (width - 1)) == (fiber_row & (width - 1))
    wanted = ((fiber_row >> log2(width)) + 1).astype(F32)
    for h in range(2):
        for copy in second[h]:
            copy.wait_recv()
        if h == 0:
            pick = (rcv2[:, 0:LANES].astype(F32) == wanted) & same_channel
            pick = jnp.transpose(pick.astype(F32))[0:group_rows, :].astype(BF16)
        begin, size = whole_down[h]
        rec[0:group_rows, lanes_of(half, h)] = jnp.dot(
            pick, rcv2[:, LANES + begin:LANES + begin + size], preferred_element_type=F32
        ).astype(BF16)
        pass_on(("D", 0), h)
        share(0, "D", h)
        square(0, lanes_of(half, h))
        if h == 0:
            to_peers[0].wait_recv()
            prepare((place_x - 1 + x_count) % x_count)

    def came(kind, j, p):
        arrivals[kind, j, p].wait_recv()
        pass_on((kind, j), p)
        share(j, kind, p)
        square(2 * j, lanes_of(which_of(kind, j), p))

    due = (
        {
            ("D", 1): 4, ("D", 2): 5, ("D", 3): 10, ("D", 4): 11, ("U", 2): 10,
            ("U", 1): 14, ("U", 3): 15, ("U", 0): 18, ("U", 4): 19,
        },
        {
            ("D", 1): 11, ("D", 2): 12, ("D", 3): 16, ("D", 4): 17, ("U", 2): 17,
            ("U", 1): 21, ("U", 3): 22, ("U", 0): 23, ("U", 4): 24,
        },
    )
    events = sorted((due[p][node], *node, p) for p in range(2) for node in parents[p])
    for count, (_, kind, j, p) in enumerate(events):
        came(kind, j, p)
        if 1 <= count < x_count - 1:
            to_peers[count].wait_recv()
            prepare((place_x - 1 - count + x_count) % x_count)
        if (kind, j, p) == ("D", links, 1):
            for t in range(1, links + 1):
                finish_odd(t, "D")
    for t in range(1, links + 1):
        finish_odd(t, "U")
    for j in range(links, -1, -1):
        finish_lent(j)

    norm = jnp.sum(norms[...], axis=1, keepdims=True)
    mask = masks[...].astype(BF16)
    tile = LANES * (1 if columns % (3 * LANES) else 3)

    def score(which):
        def multiply(index, carry):
            here = pl.ds(pl.multiple_of(index * tile, tile), tile)
            there = pl.ds(pl.multiple_of(which * segment + index * tile, LANES), tile)
            total = jnp.dot(weights[0], rec[:, there], preferred_element_type=F32)
            for s in range(1, FOLD):
                there = pl.ds(pl.multiple_of(which * segment + index * tile + s * lag, LANES), tile)
                total = total + jnp.dot(weights[s], rec[:, there], preferred_element_type=F32)
            prod[:, here] = total
            return carry

        lax.fori_loop(0, columns // tile, multiply, 0)
        there = pl.ds(pl.multiple_of(which * segment, LANES), segment + taps)
        energy = jnp.dot(mask, squares[0, :, there], preferred_element_type=F32)
        energy = energy + jnp.dot(mask, squares[1, :, there], preferred_element_type=F32)
        shift = 1
        while shift < taps:
            energy = energy + pltpu.roll(energy, energy.shape[1] - shift, 1)
            shift *= 2
        energy = energy[:, 0:segment]

        def fold(index, carry):
            part = prod[pl.ds(pl.multiple_of(index * lag, lag), lag), :]
            size = lag // 2
            while size >= 8:
                part = part[0:size, :] + pltpu.roll(part[size:, :], columns - size, 1)
                size //= 2
            for t in range(columns // LANES):
                strips[t, pl.ds(pl.multiple_of(index * 8, 8), 8), :] = part[:, t * LANES:(t + 1) * LANES]
            return carry

        lax.fori_loop(0, x_count, fold, 0)
        numer = jnp.zeros((x_count, columns), F32)
        for a in range(8):
            strip = jnp.concatenate(
                [strips[t, pl.ds(a, x_count, stride=8), :] for t in range(columns // LANES)], axis=1
            )
            numer = numer + (strip if a == 0 else pltpu.roll(strip, columns - a, 1))
        return numer[:, 0:segment] * jnp.sqrt(volume / (jnp.maximum(energy, volume) * norm))

    given[...] = score(1 - half)
    trade = send(given, taken, so, ro, partner)
    own = score(half)
    for x in range(x_count):
        out_ref[pl.ds(2 * x + half, 1), :] = own[x:x + 1, :]
    trade.wait_recv()
    for x in range(x_count):
        out_ref[pl.ds(2 * x + 1 - half, 1), :] = taken[x:x + 1, :]

    for copy in sends:
        copy.wait_send()
    for t in range(1, links + 1):
        for kind in ("D", "U"):
            for p in range(2):
                cross(t, kind, p).wait_send()
        lend_cross(t).wait_send()
    for j in range(links + 1):
        lend(j).wait_send()


def body(run, raw_stretches, stretch_ids, templates, offsets):
    chan_count = lax.axis_size("chan")
    tmpl_count = lax.axis_size("tmpl")
    slots, width, segment = raw_stretches.shape
    span, taps = templates.shape[2:]
    per_group = chan_count // 2
    group_rows = per_group * width
    reach = span // group_rows
    links = reach // 2
    rows = slots * width
    total_rows = (reach + 1) * group_rows
    lag = taps // FOLD
    columns = segment + lag
    classes = chan_count // run
    x_count = tmpl_count // 2
    homed = tmpl_count
    dma = pltpu.SemaphoreType.DMA
    vmem = pl.BlockSpec(memory_space=pltpu.VMEM)
    pairs = [dma((classes, 2))] * 2 + [dma((run, 2))] * 2 + [dma((x_count,))] * 2
    pairs += [dma((links + 1, 2))] * 8 + [dma((links + 1,))] * 4 + [dma] * 2
    detection = pl.pallas_call(
        functools.partial(kernel, chan_count, tmpl_count, run, width, per_group),
        out_shape=jax.ShapeDtypeStruct((homed, segment), F32),
        in_specs=[vmem, vmem, vmem, pl.BlockSpec(memory_space=pltpu.SMEM)],
        out_specs=vmem,
        scratch_shapes=[
            pltpu.VMEM((rows, segment + LANES), BF16),
            pltpu.VMEM((rows, segment + LANES), BF16),
            pltpu.VMEM((rows, segment + LANES), BF16),
            pltpu.VMEM((rows, segment + LANES), BF16),
            pltpu.VMEM((total_rows, 2 * segment + taps), BF16),
            pltpu.VMEM((x_count, span + 16, taps), BF16),
            pltpu.VMEM((FOLD, x_count * lag, total_rows), BF16),
            pltpu.VMEM((2, total_rows, 2 * segment + taps), BF16),
            pltpu.VMEM((x_count * lag, columns), F32),
            pltpu.VMEM((columns // LANES, x_count * 8, LANES), F32),
            pltpu.VMEM((x_count, taps), F32),
            pltpu.VMEM((x_count, total_rows), F32),
            pltpu.VMEM((x_count, segment), F32),
            pltpu.VMEM((x_count, segment), F32),
            *pairs,
        ],
        compiler_params=pltpu.CompilerParams(
            collective_id=0, has_side_effects=True, vmem_limit_bytes=48 * 1024 * 1024
        ),
    )(
        raw_stretches.reshape(rows, segment),
        stretch_ids.reshape(1, slots),
        templates.reshape(span, taps),
        offsets,
    )
    return detection.reshape(1, homed, segment)


def solution(mesh, run=8):
    placed = (P("chan", None, "tmpl"), P("chan"), P("chan", "tmpl", None, None), P("chan", "tmpl"))
    return jax.shard_map(
        functools.partial(body, run), mesh=mesh, in_specs=placed, out_specs=P("chan", None, "tmpl"), check_vma=False
    )
```

```python
import functools

import jax
import jax.numpy as jnp
from jax import lax
from jax.experimental import pallas as pl
from jax.experimental.pallas import tpu as pltpu
from jax.sharding import PartitionSpec as P

MESH = pl.DeviceIdType.MESH
F32 = jnp.float32
BF16 = jnp.bfloat16
I32 = jnp.int32
FOLD = 2
LANES = 128


def iota(shape, axis):
    return lax.broadcasted_iota(I32, shape, axis)


def log2(number):
    return number.bit_length() - 1


def kernel(
    chan_count, tmpl_count, run, width, per_group,
    raw_ref, ids_ref, tmpl_ref, off_ref, out_ref,
    snd1, rcv1, snd2, rcv2, rec, bank, weights, squares, prod, strips, norms, masks, given, taken,
    s1, r1, s2, r2, st, rt, sd, rd, su, ru, scd, rcd, scu, rcu, sfe, rfe, sfo, rfo, so, ro,
):
    rows, segment = raw_ref.shape
    span, taps = tmpl_ref.shape
    group_rows = per_group * width
    reach = span // group_rows
    links = reach // 2
    total_rows = (reach + 1) * group_rows
    columns = prod.shape[1]
    lag = taps // FOLD
    x_count = tmpl_count // 2
    classes = chan_count // run
    block1 = run * width
    block2 = classes * width
    cut = segment // 2
    volume = float(span * taps)

    chan = lax.axis_index("chan")
    tmpl = lax.axis_index("tmpl")
    core = chan % 2
    place_z = (chan // 2) % run
    place_y = chan // (2 * run)
    place_x = tmpl // 2
    half = tmpl % 2
    my_class = place_y * 2 + core
    ring = place_z + run * half
    sibling = chan + 1 - 2 * core

    def chan_of(cls, z):
        return ((cls // 2) * run + z) * 2 + cls % 2

    def half_at(place):
        return ((place + 4 * run) % (2 * run)) // run

    def x_peer(step):
        return (tmpl + 2 * step + tmpl_count) % tmpl_count

    def near(steps, move):
        return ((chan + 2 * steps + 2 * chan_count) % chan_count, place_x * 2 + half_at(ring + move))

    parents = (
        {
            ("D", 1): ("D", 0), ("D", 2): ("D", 0), ("D", 3): ("D", 2), ("D", 4): ("D", 2), ("U", 2): ("D", 0),
            ("U", 1): ("U", 2), ("U", 3): ("U", 2), ("U", 0): ("U", 1), ("U", 4): ("U", 3),
        },
        {
            ("D", 1): ("D", 0), ("D", 2): ("D", 0), ("D", 3): ("D", 2), ("D", 4): ("D", 2), ("U", 2): ("D", 0),
            ("U", 4): ("U", 2), ("U", 0): ("U", 2), ("U", 3): ("U", 2), ("U", 1): ("U", 2),
        },
    )

    def route(node, parent):
        return parent[1] - node[1], parent[1] - node[1] + (run if node[0] != parent[0] else 0)

    partner = (chan, tmpl + 1 - 2 * half)
    earlier, earlier_sibling = (chan, x_peer(-1)), (sibling, x_peer(-1))

    barrier = pltpu.get_barrier_semaphore()
    greeted = [(chan_of((my_class + d) % classes, place_z), tmpl) for d in range(1, classes)]
    greeted += [(chan_of(my_class, (place_z + d) % run), tmpl) for d in range(1, run)]
    greeted += [(chan, x_peer(d)) for d in range(1, x_count)]
    routes = {route(*link) for table in parents for link in table.items()}
    routes = sorted(routes | {(-steps, -move) for steps, move in routes})
    greeted += [near(steps, move) for steps, move in routes]
    greeted += [partner, earlier_sibling, (sibling, x_peer(1))]
    for device in reversed(greeted):
        pl.semaphore_signal(barrier, inc=1, device_id=device, device_id_type=MESH)

    bank[place_x, 0:span, :] = tmpl_ref[...]
    bank[place_x, span:, :] = jnp.full((bank.shape[1] - span, taps), off_ref[0, 0].astype(F32)).astype(BF16)

    out_row = iota((rows, rows), 0)
    in_row = iota((rows, rows), 1)
    slots = rows // width
    ids = jnp.broadcast_to(ids_ref[...], (8, slots))
    parts = jnp.where(iota((8, slots), 0) == 0, ids >> log2(per_group), ids & (per_group - 1))
    spread = iota((slots, rows), 0) == (iota((slots, rows), 1) >> log2(width))
    parts = jnp.dot(
        parts.astype(F32).astype(BF16), spread.astype(F32).astype(BF16), preferred_element_type=F32
    ).astype(I32)
    cls = out_row >> log2(block1)
    dest_z = (out_row >> log2(width)) & (run - 1)
    dest = (((cls >> 1) * run + dest_z) << 1) + (cls & 1)
    same = (in_row & (width - 1)) == (out_row & (width - 1))
    select = (parts[0:1, :] == dest) & same
    places = jnp.sum(jnp.where(select, parts[1:2, :] + 1, 0).astype(F32), axis=1, keepdims=True)
    snd1[:, LANES:] = jnp.dot(
        select.astype(F32).astype(BF16), raw_ref[...], preferred_element_type=F32
    ).astype(BF16)
    snd1[:, 0:LANES] = jnp.broadcast_to(places, (rows, LANES)).astype(BF16)

    pl.semaphore_wait(barrier, len(greeted))

    sends = []

    def copy_to(src, dst, s_sem, r_sem, device):
        return pltpu.make_async_remote_copy(
            src_ref=src, dst_ref=dst, send_sem=s_sem, recv_sem=r_sem, device_id=device, device_id_type=MESH
        )

    def send(*args):
        copy = copy_to(*args)
        copy.start()
        sends.append(copy)
        return copy

    def block(index, size):
        return pl.ds(pl.multiple_of(index * size, size), size)

    stretches = (pl.ds(0, LANES + cut), pl.ds(LANES + cut, segment - cut))
    first = [[], []]
    for h, lanes in enumerate(stretches):
        for d in range(1, classes):
            target = (my_class + d) % classes
            first[h].append(send(
                snd1.at[block(target, block1), lanes], rcv1.at[block(my_class, block1), lanes],
                s1.at[d, h], r1.at[d, h], (chan_of(target, place_z), tmpl),
            ))
    rcv1[block(my_class, block1), :] = snd1[block(my_class, block1), :]

    source = ((out_row >> log2(width)) & (classes - 1)) * block1 + (out_row >> log2(block2)) * width + (out_row & (width - 1))
    order = (in_row == source).astype(F32).astype(BF16)
    second = [[], []]
    for h, lanes in enumerate(stretches):
        for copy in first[h]:
            copy.wait_recv()
        snd2[:, lanes] = jnp.dot(order, rcv1[:, lanes], preferred_element_type=F32).astype(BF16)
        for d in range(1, run):
            target = (place_z + d) % run
            second[h].append(send(
                snd2.at[block(target, block2), lanes], rcv2.at[block(place_z, block2), lanes],
                s2.at[d, h], r2.at[d, h], (chan_of(my_class, target), tmpl),
            ))
    to_peers = [
        send(bank.at[place_x], bank.at[place_x], st.at[d], rt.at[d], (chan, x_peer(d))) for d in range(1, x_count)
    ]
    rcv2[block(place_z, block2), :] = snd2[block(place_z, block2), :]

    def prepare(index):
        template = bank[index, 0:span, :]
        offset = bank[index, span:span + 16, :].astype(F32)[0:1, 0:1].astype(I32)
        shape = (span, total_rows)
        inside = chan + (iota(shape, 1) >> log2(group_rows)) < chan_count
        moved = ((iota(shape, 1) - iota(shape, 0)) == offset) & inside
        turned = lax.dot_general(
            template, moved.astype(F32).astype(BF16), (((0,), (0,)), ((), ())), preferred_element_type=F32
        ).astype(BF16)
        for s in range(FOLD):
            weights[s, block(index, lag), :] = turned[s * lag:(s + 1) * lag, :]
        wide = template.astype(F32)
        norms[pl.ds(index, 1), :] = jnp.sum(wide * wide, axis=0, keepdims=True)
        lane = iota((1, total_rows), 1)
        covered = (lane >= offset) & (lane < offset + span) & (chan + (lane >> log2(group_rows)) < chan_count)
        masks[pl.ds(index, 1), :] = covered.astype(F32)

    def group(index):
        return pl.ds(pl.multiple_of(index * group_rows, group_rows), group_rows)

    whole_down = ((0, cut), (cut, segment - cut))
    arrivals = {}

    def lanes_of(which, p):
        return pl.ds(pl.multiple_of(which * segment + whole_down[p][0], LANES), whole_down[p][1])

    def which_of(kind, j):
        near_half = half_at(ring + j)
        return near_half if kind == "D" else 1 - near_half

    def pass_on(parent, p):
        for node in parents[p]:
            if parents[p][node] == parent:
                (kind, j), lanes = node, lanes_of(which_of(*parent), p)
                s_sem, r_sem = {"D": (sd, rd), "U": (su, ru)}[kind]
                arrivals[kind, j, p] = send(
                    rec.at[group(2 * parent[1]), lanes], rec.at[group(2 * j), lanes], s_sem.at[j, p], r_sem.at[j, p],
                    near(*route(node, parent)),
                )

    def cross(t, kind, p):
        j = t - core
        lanes = lanes_of(which_of(kind, j), p)
        s_sem, r_sem = {"D": (scd, rcd), "U": (scu, rcu)}[kind]
        return copy_to(
            rec.at[group(2 * j), lanes], rec.at[group(2 * t - 1), lanes], s_sem.at[t, p], r_sem.at[t, p],
            (sibling, tmpl),
        )

    tail = pl.ds(2 * segment, taps)

    def lend(j):
        return copy_to(rec.at[group(2 * j), 0:taps], rec.at[group(2 * j), tail], sfe.at[j], rfe.at[j], earlier)

    def lend_cross(t):
        return copy_to(
            rec.at[group(2 * (t - core)), 0:taps], rec.at[group(2 * t - 1), tail], sfo.at[t], rfo.at[t],
            earlier_sibling,
        )

    def share(j, kind, p):
        which = which_of(kind, j)
        t = j + core
        inner = 1 <= j < links
        if inner:
            cross(t, kind, p).start()
        else:
            @pl.when(core == (1 if j == 0 else 0))
            def _():
                cross(t, kind, p).start()

        if p == 0:
            @pl.when(which == 0)
            def _():
                lend(j).start()
                if inner:
                    lend_cross(t).start()

            if not inner:
                @pl.when((which == 0) & (core == (1 if j == 0 else 0)))
                def _():
                    lend_cross(t).start()

    last = place_x == x_count - 1

    def square(index, lanes):
        value = rec[group(index), lanes].astype(F32)
        squared = value * value
        high = squared.astype(BF16)
        squares[0, group(index), lanes] = high
        squares[1, group(index), lanes] = (squared - high.astype(F32)).astype(BF16)

    def square_tail(index):
        @pl.when(last)
        def _():
            rec[group(index), tail] = jnp.zeros((group_rows, taps), BF16)

        square(index, tail)

    def finish_odd(t, kind):
        for p in range(2):
            copy = cross(t, kind, p)
            copy.wait_recv()
            square(2 * t - 1, lanes_of(which_of(kind, t - 1 + core), p))

    def finish_lent(j):
        lend(j).wait_recv()
        square_tail(2 * j)
        if j > 0:
            lend_cross(j).wait_recv()
            square_tail(2 * j - 1)

    prepare(place_x)
    arrived_rows = iota((rows, LANES), 0)
    fiber_row = iota((rows, LANES), 1)
    same_channel = (arrived_rows & (width - 1)) == (fiber_row & (width - 1))
    wanted = ((fiber_row >> log2(width)) + 1).astype(F32)
    for h in range(2):
        for copy in second[h]:
            copy.wait_recv()
        if h == 0:
            pick = (rcv2[:, 0:LANES].astype(F32) == wanted) & same_channel
            pick = jnp.transpose(pick.astype(F32))[0:group_rows, :].astype(BF16)
        begin, size = whole_down[h]
        rec[0:group_rows, lanes_of(half, h)] = jnp.dot(
            pick, rcv2[:, LANES + begin:LANES + begin + size], preferred_element_type=F32
        ).astype(BF16)
        pass_on(("D", 0), h)
        share(0, "D", h)
        square(0, lanes_of(half, h))
        if h == 0:
            to_peers[0].wait_recv()
            prepare((place_x - 1 + x_count) % x_count)

    def came(kind, j, p):
        arrivals[kind, j, p].wait_recv()
        pass_on((kind, j), p)
        share(j, kind, p)
        square(2 * j, lanes_of(which_of(kind, j), p))

    due = (
        {
            ("D", 1): 4, ("D", 2): 5, ("D", 3): 10, ("D", 4): 11, ("U", 2): 10,
            ("U", 1): 14, ("U", 3): 15, ("U", 0): 18, ("U", 4): 19,
        },
        {
            ("D", 1): 11, ("D", 2): 12, ("D", 3): 16, ("D", 4): 17, ("U", 2): 17,
            ("U", 1): 21, ("U", 3): 22, ("U", 0): 23, ("U", 4): 24,
        },
    )
    events = sorted((due[p][node], *node, p) for p in range(2) for node in parents[p])
    for count, (_, kind, j, p) in enumerate(events):
        came(kind, j, p)
        if 1 <= count < x_count - 1:
            to_peers[count].wait_recv()
            prepare((place_x - 1 - count + x_count) % x_count)
        if (kind, j, p) == ("D", links, 1):
            for t in range(1, links + 1):
                finish_odd(t, "D")
    for t in range(1, links + 1):
        finish_odd(t, "U")
    for j in range(links, -1, -1):
        finish_lent(j)

    norm = jnp.sum(norms[...], axis=1, keepdims=True)
    mask = masks[...].astype(BF16)
    tile = LANES * (1 if columns % (3 * LANES) else 3)

    def score(which):
        def multiply(index, carry):
            here = pl.ds(pl.multiple_of(index * tile, tile), tile)
            there = pl.ds(pl.multiple_of(which * segment + index * tile, LANES), tile)
            total = jnp.dot(weights[0], rec[:, there], preferred_element_type=F32)
            for s in range(1, FOLD):
                there = pl.ds(pl.multiple_of(which * segment + index * tile + s * lag, LANES), tile)
                total = total + jnp.dot(weights[s], rec[:, there], preferred_element_type=F32)
            prod[:, here] = total
            return carry

        lax.fori_loop(0, columns // tile, multiply, 0)
        there = pl.ds(pl.multiple_of(which * segment, LANES), segment + taps)
        energy = jnp.dot(mask, squares[0, :, there], preferred_element_type=F32)
        energy = energy + jnp.dot(mask, squares[1, :, there], preferred_element_type=F32)
        shift = 1
        while shift < taps:
            energy = energy + pltpu.roll(energy, energy.shape[1] - shift, 1)
            shift *= 2
        energy = energy[:, 0:segment]

        def fold(index, carry):
            part = prod[pl.ds(pl.multiple_of(index * lag, lag), lag), :]
            size = lag // 2
            while size >= 8:
                part = part[0:size, :] + pltpu.roll(part[size:, :], columns - size, 1)
                size //= 2
            for t in range(columns // LANES):
                strips[t, pl.ds(pl.multiple_of(index * 8, 8), 8), :] = part[:, t * LANES:(t + 1) * LANES]
            return carry

        lax.fori_loop(0, x_count, fold, 0)
        numer = jnp.zeros((x_count, columns), F32)
        for a in range(8):
            strip = jnp.concatenate(
                [strips[t, pl.ds(a, x_count, stride=8), :] for t in range(columns // LANES)], axis=1
            )
            numer = numer + (strip if a == 0 else pltpu.roll(strip, columns - a, 1))
        return numer[:, 0:segment] * jnp.sqrt(volume / (jnp.maximum(energy, volume) * norm))

    given[...] = score(1 - half)
    trade = send(given, taken, so, ro, partner)
    own = score(half)
    for x in range(x_count):
        out_ref[pl.ds(2 * x + half, 1), :] = own[x:x + 1, :]
    trade.wait_recv()
    for x in range(x_count):
        out_ref[pl.ds(2 * x + 1 - half, 1), :] = taken[x:x + 1, :]

    for copy in sends:
        copy.wait_send()
    for t in range(1, links + 1):
        for kind in ("D", "U"):
            for p in range(2):
                cross(t, kind, p).wait_send()
        lend_cross(t).wait_send()
    for j in range(links + 1):
        lend(j).wait_send()


def body(run, raw_stretches, stretch_ids, templates, offsets):
    chan_count = lax.axis_size("chan")
    tmpl_count = lax.axis_size("tmpl")
    slots, width, segment = raw_stretches.shape
    span, taps = templates.shape[2:]
    per_group = chan_count // 2
    group_rows = per_group * width
    reach = span // group_rows
    links = reach // 2
    rows = slots * width
    total_rows = (reach + 1) * group_rows
    lag = taps // FOLD
    columns = segment + lag
    classes = chan_count // run
    x_count = tmpl_count // 2
    homed = tmpl_count
    dma = pltpu.SemaphoreType.DMA
    vmem = pl.BlockSpec(memory_space=pltpu.VMEM)
    pairs = [dma((classes, 2))] * 2 + [dma((run, 2))] * 2 + [dma((x_count,))] * 2
    pairs += [dma((links + 1, 2))] * 8 + [dma((links + 1,))] * 4 + [dma] * 2
    detection = pl.pallas_call(
        functools.partial(kernel, chan_count, tmpl_count, run, width, per_group),
        out_shape=jax.ShapeDtypeStruct((homed, segment), F32),
        in_specs=[vmem, vmem, vmem, pl.BlockSpec(memory_space=pltpu.SMEM)],
        out_specs=vmem,
        scratch_shapes=[
            pltpu.VMEM((rows, segment + LANES), BF16),
            pltpu.VMEM((rows, segment + LANES), BF16),
            pltpu.VMEM((rows, segment + LANES), BF16),
            pltpu.VMEM((rows, segment + LANES), BF16),
            pltpu.VMEM((total_rows, 2 * segment + taps), BF16),
            pltpu.VMEM((x_count, span + 16, taps), BF16),
            pltpu.VMEM((FOLD, x_count * lag, total_rows), BF16),
            pltpu.VMEM((2, total_rows, 2 * segment + taps), BF16),
            pltpu.VMEM((x_count * lag, columns), F32),
            pltpu.VMEM((columns // LANES, x_count * 8, LANES), F32),
            pltpu.VMEM((x_count, taps), F32),
            pltpu.VMEM((x_count, total_rows), F32),
            pltpu.VMEM((x_count, segment), F32),
            pltpu.VMEM((x_count, segment), F32),
            *pairs,
        ],
        compiler_params=pltpu.CompilerParams(
            collective_id=0, has_side_effects=True, vmem_limit_bytes=48 * 1024 * 1024
        ),
    )(
        raw_stretches.reshape(rows, segment),
        stretch_ids.reshape(1, slots),
        templates.reshape(span, taps),
        offsets,
    )
    return detection.reshape(1, homed, segment)


def solution(mesh, run=8):
    placed = (P("chan", None, "tmpl"), P("chan"), P("chan", "tmpl", None, None), P("chan", "tmpl"))
    return jax.shard_map(
        functools.partial(body, run), mesh=mesh, in_specs=placed, out_specs=P("chan", None, "tmpl"), check_vma=False
    )
```
